32 devices in a mesh: groups: 2 (over x), dp: 2 (over core), tensor: 8 (over z, y).
Axes of the slice: x: 2, y: 2, z: 4, core: 2. Of those that a mesh axis runs over, the one named last changes fastest.
Arguments:
- gate_preactivation: bfloat16 [3072, 14336], P(('groups', 'dp'), 'tensor'), parts along dimension 0, may hold values from -6 to 6
- up_preactivation: bfloat16 [3072, 14336], P(('groups', 'dp'), 'tensor'), parts along dimension 0, may hold values from -6 to 6
- base_down_matrix: bfloat16 [14336, 8192], P('tensor'), may hold values from -0.0625 to 0.0625
- adapter_first_factor: bfloat16 [64, 14336, 64], P('dp', 'tensor'), may hold values from -0.046875 to 0.046875
- adapter_second_factor: bfloat16 [64, 64, 8192], P('dp', None, 'tensor'), may hold values from -0.75 to 0.75
- residual: bfloat16 [3072, 8192], P(('groups', 'dp'), 'tensor'), parts along dimension 0
- scoring_head_matrix: float32 [8192], replicated, may hold values from -0.0625 to 0.0625
- block_adapter_index: int32 [24], P('groups'), parts along dimension 0, may hold values from 0 to 63
- block_span_start: int32 [24], P(('groups', 'dp')), parts along dimension 0, may hold values from 0 to 127, as said below
- block_span_end: int32 [24], P(('groups', 'dp')), parts along dimension 0, may hold values from 1 to 128, as said below
Outputs:
- layer_out: bfloat16 [3072, 8192], P(('groups', 'dp'), 'tensor'), parts along dimension 0
- span_scores: float32 [24], P(('groups', 'dp')), parts along dimension 0
The draws below stay inside these ranges and needn't reach their ends.
There are 2 independent parts, one for each index of `groups`. The reference program is written for one: setup_inputs(seed, part) draws one part's arguments, and reference() takes and returns one part's arrays. A program takes and returns all parts, laid end to end along the dimension named above; an argument that names none is the same for every part. Nothing has to cross between parts.
Inputs may be any that keep to these rules, and one draw needn't show every extreme that they name: Each block's scored positions satisfy 0 <= block_span_start < block_span_end <= 128. block_span_end is greater than block_span_start of the same block.
All inputs are finite; a program needn't handle non-finite values.
Results may differ from the reference program's by a relative error of at most 0.0049.
Values may be sent and summed in bfloat16 or wider, within the bound.
No kernel may reach another device: no remote copies, remote signals or barrier semaphores. Data moves between devices by JAX's collectives and lax.ppermute only.
A program may use at most 192 MiB of HBM per device.

```python
import math
import jax
import jax.numpy as jnp
import numpy as np
from jax import lax

MODEL_WIDTH = 8192
HIDDEN_HALF = 14336
ADAPTER_RANK = 64
ADAPTER_COUNT = 64
BLOCK = 128
BLOCKS = 12
ROWS = 1536


def span_bounds(key):
    lower_key, upper_key, first_key, second_key = jax.random.split(jax.random.fold_in(key, 5), 4)
    lower_pick = jax.random.randint(lower_key, (BLOCKS,), 0, BLOCK, dtype=jnp.int32)
    upper_pick = jax.random.randint(upper_key, (BLOCKS,), 0, BLOCK, dtype=jnp.int32)
    starts = jnp.minimum(lower_pick, upper_pick)
    ends = jnp.maximum(lower_pick, upper_pick) + 1
    late_block = jax.random.randint(first_key, (), 0, BLOCKS, dtype=jnp.int32)
    early_block = (late_block + 1 + jax.random.randint(second_key, (), 0, BLOCKS - 1, dtype=jnp.int32)) % BLOCKS
    blocks = jnp.arange(BLOCKS, dtype=jnp.int32)
    starts = jnp.where(blocks == late_block, BLOCK - 1, starts)
    ends = jnp.where(blocks == late_block, BLOCK, ends)
    starts = jnp.where(blocks == early_block, 0, starts)
    ends = jnp.where(blocks == early_block, 1, ends)
    return (starts.astype(jnp.int32), ends.astype(jnp.int32))


def draw_block_span_start(key, part):
    return span_bounds(key)[0]


def draw_block_span_end(key, part):
    return span_bounds(key)[1]


def draw_residual(key, part):
    key = jax.random.fold_in(key, 11)
    noise_key, row_key, column_key = jax.random.split(key, 3)
    gaussian = jax.random.normal(noise_key, (ROWS, MODEL_WIDTH), jnp.float32)
    column = jnp.arange(MODEL_WIDTH, dtype=jnp.float32) / MODEL_WIDTH
    row_scale = jax.random.uniform(row_key, (ROWS, 1), jnp.float32, 0.6, 1.4)
    column_scale = jax.random.uniform(column_key, (1, MODEL_WIDTH), jnp.float32, 0.7, 1.3) * 3.0 ** column[None, :]
    values = 0.5 * gaussian * row_scale * column_scale
    return jnp.clip(values, -8.0, 8.0).astype(jnp.bfloat16)


def place_ends(result, own_key, low, high):
    longest = result.shape.index(max(result.shape))
    spots = []
    for shift in (0, 1):
        where = [jax.random.randint(jax.random.fold_in(own_key, axis), (), 0, length) for axis, length in enumerate(result.shape)]
        where[longest] = (where[longest] + shift) % result.shape[longest]
        spots.append(tuple(where))
    return result.at[spots[0]].set(low).at[spots[1]].set(high)


def raised(result, own_key, source, target, shards_of, factor):
    def block_of(dim):
        return (jnp.arange(result.shape[dim]) // (result.shape[dim] // shards_of)).reshape((-1,) + (1,) * (result.ndim - 1 - dim))

    one_side = jax.random.permutation(own_key, shards_of)[block_of(target)]
    far = (block_of(target) + shards_of // 2) % shards_of
    return jnp.where((block_of(source) == one_side) | (block_of(source) == far), factor * result, result)


def steps_of(stream_key, extent, cuts, least, high):
    loudness, own = 1.0, jax.random.fold_in(stream_key, 6)
    for axis_at, blocks in cuts:
        heights = jnp.exp(jax.random.uniform(jax.random.fold_in(own, axis_at), (blocks,), jnp.float32, least / len(cuts), high / len(cuts)))
        loudness = loudness * jnp.repeat(heights, extent[axis_at] // blocks).reshape([-1 if axis == axis_at else 1 for axis in range(len(extent))])
    return loudness


def rank_bounds(count, slope):
    portions = [(1 << 20) // math.isqrt(rank ** slope) + 1 for rank in range(1, count + 1)]
    spread = 1 + sum(portions) // (1 << 30)
    return np.cumsum(np.array([max(1, weight // spread) for weight in portions]))


def ranked_ids(stream_key, extent, amount, skew):
    table = rank_bounds(amount, skew)
    ticket = jax.random.randint(jax.random.fold_in(stream_key, 1), extent, 0, int(table[amount - 1]))
    grade = jnp.searchsorted(jnp.asarray(table, jnp.int32), ticket, side="right")
    return jax.random.permutation(jax.random.fold_in(stream_key, 2), amount)[grade].astype(jnp.int32)


def normal_values(stream_key, dims, scale, limit, cuts=(), kind=jnp.bfloat16):
    values = jax.random.normal(stream_key, dims, jnp.float32) * scale
    if len(cuts) > 0:
        values = steps_of(stream_key, dims, cuts, -0.22, 0.18) * values
    return jnp.clip(values, min=-limit, max=limit).astype(kind)


def heavy_noise(own_key, shape, width, limit, pieces, heavy, kind=jnp.bfloat16):
    drawn = width * jax.random.normal(own_key, shape, jnp.float32)
    if pieces:
        drawn = drawn * steps_of(own_key, shape, pieces, -0.22, 0.18)
    return jnp.clip(raised(drawn, jax.random.fold_in(own_key, 3), *heavy), -limit, limit).astype(kind)


def setup_inputs(seed: int = 0, part: int = 0) -> dict:
    splits = jax.random.split(jax.random.key(seed), 11)
    part_splits = jax.random.split(jax.random.fold_in(splits[10], part), 11)
    return {
        "gate_preactivation": normal_values(part_splits[0], (ROWS, HIDDEN_HALF), 1.0, 6.0, ((0, 2), (1, 8))),
        "up_preactivation": normal_values(part_splits[1], (ROWS, HIDDEN_HALF), 1.0, 6.0, ((0, 2), (1, 8))),
        "base_down_matrix": heavy_noise(splits[2], (HIDDEN_HALF, MODEL_WIDTH), HIDDEN_HALF ** -0.5, 0.0625, ((0, 8),), (0, 1, 8, 2.0)),
        "adapter_first_factor": normal_values(splits[3], (ADAPTER_COUNT, HIDDEN_HALF, ADAPTER_RANK), HIDDEN_HALF ** -0.5, 0.046875, ((0, 2), (1, 8))),
        "adapter_second_factor": normal_values(splits[4], (ADAPTER_COUNT, ADAPTER_RANK, MODEL_WIDTH), ADAPTER_RANK ** -0.5, 0.75, ((0, 2), (2, 8))),
        "residual": draw_residual(jax.random.fold_in(jax.random.fold_in(splits[10], part), 71), part),
        "scoring_head_matrix": normal_values(splits[6], (MODEL_WIDTH,), MODEL_WIDTH ** -0.5, 0.0625, (), jnp.float32),
        "block_adapter_index": place_ends(ranked_ids(part_splits[7], (BLOCKS,), ADAPTER_COUNT, 2), jax.random.fold_in(part_splits[7], 3), 0, ADAPTER_COUNT - 1).astype(jnp.int32),
        "block_span_start": draw_block_span_start(jax.random.fold_in(jax.random.fold_in(splits[10], part), 71), part),
        "block_span_end": draw_block_span_end(jax.random.fold_in(jax.random.fold_in(splits[10], part), 71), part),
    }


epsilon = 1e-05

def reference(gate_preactivation, up_preactivation, base_down_matrix, adapter_first_factor, adapter_second_factor, residual, scoring_head_matrix, block_adapter_index, block_span_start, block_span_end):
    hidden = (jax.nn.silu(gate_preactivation.astype(jnp.float32)) * up_preactivation.astype(jnp.float32)).astype(jnp.bfloat16)
    base_part = jnp.dot(hidden, base_down_matrix, preferred_element_type=jnp.float32)
    hidden_blocks = hidden.reshape(BLOCKS, BLOCK, HIDDEN_HALF).astype(jnp.float32)
    selected_down_factor = adapter_first_factor[block_adapter_index].astype(jnp.float32)
    low_rank_update = jnp.einsum('kbf,kfr->kbr', hidden_blocks, selected_down_factor).astype(jnp.bfloat16)
    low_rank_update = lax.optimization_barrier(low_rank_update).astype(jnp.float32)
    selected_up_factor = adapter_second_factor[block_adapter_index].astype(jnp.float32)
    adapter_delta = jnp.einsum('kbr,krd->kbd', low_rank_update, selected_up_factor).astype(jnp.bfloat16)
    adapter_delta = lax.optimization_barrier(adapter_delta).astype(jnp.float32).reshape(ROWS, MODEL_WIDTH)
    combined = residual.astype(jnp.float32) + base_part + adapter_delta
    square_sum = lax.optimization_barrier(jnp.sum(combined * combined, 1))
    head_sum = lax.optimization_barrier(jnp.sum(combined * scoring_head_matrix[None, :], 1))
    per_row = head_sum * lax.rsqrt(square_sum / MODEL_WIDTH + epsilon)
    position = jnp.arange(BLOCK, dtype=jnp.int32)
    inside = (position[None, :] >= block_span_start[:, None]) & (position[None, :] < block_span_end[:, None])
    span_scores = lax.optimization_barrier(jnp.sum(jnp.where(inside, per_row.reshape(BLOCKS, BLOCK), jnp.float32(0.0)), 1))
    return (combined.astype(jnp.bfloat16), span_scores)
```

```python
import jax
import jax.numpy as jnp
from jax import lax
from jax.sharding import PartitionSpec as P

BLOCK = 128
EPSILON = 1e-05

f32 = jnp.float32
bf16 = jnp.bfloat16

LINE = 4
PAIR = 2
ORDER = ((3, 2, 1, 0), (3, 0, 2, 1), (0, 3, 1, 2), (0, 1, 2, 3))


def along_line(value, hops):
    pairs = [(a * PAIR + y, b * PAIR + y) for a, b in hops for y in range(PAIR)]
    return lax.ppermute(value, "tensor", pairs)


def across(value, bit):
    size = LINE * PAIR
    return lax.ppermute(value, "tensor", [(t, t ^ bit) for t in range(size)])


def line_sum(parts, z):
    first = along_line(parts[0].astype(bf16), [(0, 1), (3, 2)])
    at_end = (z == 0) | (z == LINE - 1)
    second = (jnp.where(at_end, parts[1], parts[0]) + first.astype(f32)).astype(bf16)
    up = along_line(second, [(0, 1), (1, 2)])
    down = along_line(second, [(3, 2), (2, 1)])
    low = z < LINE // 2
    third_up = (jnp.where(low, parts[2], parts[1]) + up.astype(f32)).astype(bf16)
    third_down = (jnp.where(low, parts[1], parts[2]) + down.astype(f32)).astype(bf16)
    up = along_line(third_up, [(0, 1), (1, 2), (2, 3)])
    down = along_line(third_down, [(3, 2), (2, 1), (1, 0)])
    return parts[3] + up.astype(f32) + down.astype(f32)


def grid_scatter(hidden, weights, width, tensor_index):
    z, y = tensor_index // PAIR, tensor_index % PAIR
    order = jnp.asarray(ORDER, jnp.int32)[z]
    depth = weights.shape[0]

    def product(rows, column):
        block = lax.dynamic_slice(weights, (0, column * width), (depth, width))
        return jnp.dot(rows, block, preferred_element_type=f32)

    sums = []
    for k in range(LINE):
        theirs = product(hidden, order[k] * PAIR + 1 - y).astype(bf16)
        arrived = across(theirs, 1)
        mine = product(hidden, order[k] * PAIR + y)
        sums.append(mine + arrived.astype(f32))
    return line_sum(sums, z)


def exchange_sum(value, wire):
    for bit in (1, 2, 4):
        value = value + across(value.astype(wire), bit).astype(f32)
    return value


def shards(
    gate_preactivation,
    up_preactivation,
    base_down_matrix,
    adapter_first_factor,
    adapter_second_factor,
    residual,
    scoring_head_matrix,
    block_adapter_index,
    block_span_start,
    block_span_end,
):
    rows_local, hidden_width = gate_preactivation.shape
    slice_width = residual.shape[1]
    model_width = scoring_head_matrix.shape[0]
    blocks = rows_local // BLOCK
    adapters_here = adapter_first_factor.shape[0]
    data_index = lax.axis_index("dp")
    data_size = lax.axis_size("dp")
    tensor_index = lax.axis_index("tensor")
    on_grid = lax.axis_size("tensor") == LINE * PAIR

    ids = block_adapter_index.reshape(data_size, blocks)
    own_ids = lax.dynamic_index_in_dim(ids, data_index, 0, keepdims=False)
    owner = own_ids // adapters_here

    def fetched(factors):
        def held(which):
            at = jnp.clip(which - data_index * adapters_here, 0, adapters_here - 1)
            return factors[at]

        result = held(own_ids)
        for step in range(1, data_size):
            there = (data_index + step) % data_size
            wanted = held(lax.dynamic_index_in_dim(ids, there, 0, keepdims=False))
            came = lax.ppermute(
                wanted, "dp", [(d, (d + step) % data_size) for d in range(data_size)]
            )
            source = (data_index - step) % data_size
            result = jnp.where((owner == source)[:, None, None], came, result)
        return result

    first_factors = fetched(adapter_first_factor)
    second_factors = fetched(adapter_second_factor)

    hidden = (
        jax.nn.silu(gate_preactivation.astype(f32)) * up_preactivation.astype(f32)
    ).astype(bf16)
    low_rank = jnp.einsum(
        "bcj,bje->bce",
        hidden.reshape(blocks, BLOCK, hidden_width),
        first_factors,
        preferred_element_type=f32,
    ).reshape(rows_local, -1)
    if on_grid:
        low_rank = exchange_sum(low_rank, f32)
    else:
        low_rank = lax.psum(low_rank, "tensor")
    delta = jnp.einsum(
        "bcn,bnt->bct",
        low_rank.astype(bf16).reshape(blocks, BLOCK, -1),
        second_factors,
        preferred_element_type=f32,
    ).reshape(rows_local, slice_width)
    delta = delta.astype(bf16).astype(f32)

    if on_grid:
        base_part = grid_scatter(hidden, base_down_matrix, slice_width, tensor_index)
    else:
        base_part = lax.psum_scatter(
            jnp.dot(hidden, base_down_matrix, preferred_element_type=f32),
            "tensor",
            scatter_dimension=1,
            tiled=True,
        )
    combined = residual.astype(f32) + base_part + delta
    layer_out = combined.astype(bf16)
    head = lax.dynamic_slice_in_dim(
        scoring_head_matrix, tensor_index * slice_width, slice_width
    )
    stats = jnp.stack([jnp.sum(combined * combined, 1), jnp.sum(combined * head[None, :], 1)])
    stats = stats.reshape(2 * blocks, BLOCK)
    stats = exchange_sum(stats, f32) if on_grid else lax.psum(stats, "tensor")
    square_sum, head_sum = stats[:blocks], stats[blocks:]
    scores = head_sum * lax.rsqrt(square_sum / model_width + EPSILON)
    position = jnp.arange(BLOCK, dtype=jnp.int32)
    inside = (position[None, :] >= block_span_start[:, None]) & (
        position[None, :] < block_span_end[:, None]
    )
    span_scores = jnp.sum(jnp.where(inside, scores, f32(0.0)), 1)
    return (layer_out, span_scores)


def solution(mesh):
    return jax.shard_map(
        shards,
        mesh=mesh,
        in_specs=(
            P(("groups", "dp"), "tensor"),
            P(("groups", "dp"), "tensor"),
            P("tensor", None),
            P("dp", "tensor", None),
            P("dp", None, "tensor"),
            P(("groups", "dp"), "tensor"),
            P(),
            P("groups"),
            P(("groups", "dp")),
            P(("groups", "dp")),
        ),
        out_specs=(P(("groups", "dp"), "tensor"), P(("groups", "dp"))),
        check_vma=False,
    )
```

```python
import jax
import jax.numpy as jnp
from jax import lax
from jax.experimental import pallas as pl
from jax.experimental.pallas import tpu as pltpu
from jax.sharding import PartitionSpec as P

BLOCK = 128
EPSILON = 1e-05

f32 = jnp.float32
bf16 = jnp.bfloat16

LINE = 4
PAIR = 2
ORDER = ((3, 2, 1, 0), (0, 3, 2, 1), (1, 0, 3, 2), (0, 1, 2, 3))
PIECES = (3, 3)
TILE = 512


def along_line(value, hops):
    pairs = [(a * PAIR + y, b * PAIR + y) for a, b in hops for y in range(PAIR)]
    return lax.ppermute(value, "tensor", pairs)


def across(value, bit):
    size = LINE * PAIR
    return lax.ppermute(value, "tensor", [(t, t ^ bit) for t in range(size)])


class Sequence:
    def __init__(self):
        self.last = None

    def __call__(self, stage, *values):
        if self.last is not None:
            values = lax.optimization_barrier((self.last,) + values)[1:]
        result = stage(*values)
        self.last = jax.tree.leaves(result)[0]
        return result


def product_kernel(cuts, index_ref, rows_ref, weights_ref, *out_refs):
    result = jnp.dot(rows_ref[...], weights_ref[...], preferred_element_type=f32)
    for ref, start, stop in zip(out_refs, cuts[:-1], cuts[1:]):
        ref[...] = result[start:stop].astype(ref.dtype)


def product(hidden, weights, tensor_index, turn, own, kinds, width):
    rows, depth = hidden.shape
    steps = width // TILE
    cuts = [0]
    for piece in PIECES:
        cuts.append(cuts[-1] + piece * BLOCK)

    def block(j, index):
        z, y = index[0] >> 1, index[0] & 1
        goal = ORDER[LINE - 1][turn]
        for other in range(LINE - 1):
            goal = jnp.where(z == other, ORDER[other][turn], goal)
        return (goal * PAIR + (y if own else 1 - y)) * steps + j

    sizes = [stop - start for start, stop in zip(cuts[:-1], cuts[1:])]
    return pl.pallas_call(
        lambda *refs: product_kernel(cuts, *refs),
        grid_spec=pltpu.PrefetchScalarGridSpec(
            num_scalar_prefetch=1,
            grid=(steps,),
            in_specs=[
                pl.BlockSpec((rows, depth), lambda j, index: (0, 0)),
                pl.BlockSpec((depth, TILE), lambda j, index: (0, block(j, index))),
            ],
            out_specs=[pl.BlockSpec((size, TILE), lambda j, index: (0, j)) for size in sizes],
        ),
        out_shape=[jax.ShapeDtypeStruct((size, width), kind) for size, kind in zip(sizes, kinds)],
        compiler_params=pltpu.CompilerParams(vmem_limit_bytes=40 * 1024 * 1024),
        cost_estimate=pl.CostEstimate(
            flops=0,
            bytes_accessed=0,
            transcendentals=0,
        ),
    )(tensor_index.reshape(1), hidden, weights)


def pick_kernel(count, ids_ref, *refs):
    sources, targets = refs[:2], refs[2:]
    step = pl.program_id(0)

    @pl.when(step < count)
    def _():
        for source, target in zip(sources, targets[:2]):
            target[...] = source[...]

    @pl.when(step >= count)
    def _():
        for source, target in zip(sources, targets[2:]):
            target[...] = source[...]


def pick(ids, count, first, second):
    both = (first, second)
    rest = ids.shape[0] - count
    shapes = [(n,) + f.shape[1:] for n in (count, rest) for f in both]
    spot = lambda n, ids: (jnp.minimum(n, count - 1), 0, 0)
    later = lambda n, ids: (jnp.maximum(n - count, 0), 0, 0)
    return pl.pallas_call(
        lambda *refs: pick_kernel(count, *refs),
        grid_spec=pltpu.PrefetchScalarGridSpec(
            num_scalar_prefetch=1,
            grid=(count + rest,),
            in_specs=[pl.BlockSpec((1,) + f.shape[1:], lambda n, ids: (ids[n], 0, 0)) for f in both],
            out_specs=[pl.BlockSpec((1,) + s[1:], m) for s, m in zip(shapes, (spot, spot, later, later))],
        ),
        out_shape=[jax.ShapeDtypeStruct(s, first.dtype) for s in shapes],
        cost_estimate=pl.CostEstimate(flops=0, bytes_accessed=0, transcendentals=0),
    )(ids, first, second)


def exchange_sum(value, wire):
    for bit in (1, 2, 4):
        value = value + across(value.astype(wire), bit).astype(f32)
    return value


UP = ((0, 1), (1, 2), (2, 3))
DOWN = ((3, 2), (2, 1), (1, 0))


def grid_sums(hidden, weights, tensor_index, width, low_rank_terms, adapter_delta):
    last_z = (tensor_index >> 1) == LINE - 1
    then = Sequence()
    pieces = range(len(PIECES))
    arrived, mine = {}, {}
    add = lambda *terms: sum(t.astype(f32) for t in terms)
    narrow = lambda *terms: add(*terms).astype(bf16)

    def theirs(k):
        kinds = [bf16] * len(PIECES)
        out = then(lambda h: product(h, weights, tensor_index, k, False, kinds, width), hidden)
        for p in pieces:
            arrived[p, k] = across(out[p], 1)

    def ours(k):
        kinds = [f32] * len(PIECES)
        out = then(lambda h: product(h, weights, tensor_index, k, True, kinds, width), hidden)
        for p in pieces:
            mine[p, k] = out[p]

    def part(p, k):
        return (mine[p, k], arrived[p, k])

    first, second, third = {}, {}, {}

    def hop_1(p):
        first[p] = along_line(then(narrow, *part(p, 0)), [UP[0], DOWN[0]])

    def hop_2(p):
        value = then(narrow, *part(p, 1), first[p])
        second[p] = (along_line(value, UP[:2]), along_line(value, DOWN[:2]))

    def hop_3(p):
        up, down = second[p]

        def stage(up, down, *parts):
            here, there = add(*parts[:2]), add(*parts[2:])
            return narrow(here, up), narrow(jnp.where(last_z, here, there), down)

        up, down = then(stage, up, down, *part(p, 2), *part(p, 0))
        third[p] = (along_line(up, UP), along_line(down, DOWN))

    theirs(0)
    low_rank = then(low_rank_terms, hidden)
    arriving = across(low_rank, 2)
    ours(0)
    low_rank = then(add, low_rank, arriving)
    arriving = across(low_rank, 4)
    ours(1)
    low_rank = then(add, low_rank, arriving)
    arriving = across(low_rank, 1)
    theirs(1)
    hop_1(0)
    theirs(2)
    hop_1(1)
    low_rank = then(add, low_rank, arriving)
    delta = then(adapter_delta, low_rank)
    ours(2)
    hop_2(0)
    theirs(3)
    hop_2(1)
    ours(3)
    hop_3(0)
    hop_3(1)
    return jnp.concatenate([add(*part(p, 3), *third[p]) for p in pieces], 0), delta


def shards(
    gate_preactivation,
    up_preactivation,
    base_down_matrix,
    adapter_first_factor,
    adapter_second_factor,
    residual,
    scoring_head_matrix,
    block_adapter_index,
    block_span_start,
    block_span_end,
):
    rows_local, hidden_width = gate_preactivation.shape
    slice_width = residual.shape[1]
    model_width = scoring_head_matrix.shape[0]
    blocks = rows_local // BLOCK
    adapters_here = adapter_first_factor.shape[0]
    data_index = lax.axis_index("dp")
    data_size = lax.axis_size("dp")
    tensor_index = lax.axis_index("tensor")
    on_grid = lax.axis_size("tensor") == LINE * PAIR

    ids = block_adapter_index.reshape(data_size, blocks)
    owner = lax.dynamic_index_in_dim(ids, data_index, 0, keepdims=False) // adapters_here
    first_turned = jnp.swapaxes(adapter_first_factor, 1, 2)
    steps = [step for step in range(1, data_size)] + [0]
    turned = jnp.concatenate(
        [lax.dynamic_slice_in_dim(ids, (data_index + step) % data_size, 1)[0] for step in steps]
    )
    turned = jnp.clip(turned - data_index * adapters_here, 0, adapters_here - 1)
    away = blocks * (data_size - 1)
    wanted_first, wanted_second, first_factors, second_factors = pick(
        turned, away, first_turned, adapter_second_factor
    )
    for n, step in enumerate(steps[:-1]):
        hop = [(d, (d + step) % data_size) for d in range(data_size)]
        take = (owner == (data_index - step) % data_size)[:, None, None]

        def fetched(wanted, kept):
            came = lax.ppermute(wanted[n * blocks : (n + 1) * blocks], "dp", hop)
            return jnp.where(take, came, kept)

        first_factors = fetched(wanted_first, first_factors)
        second_factors = fetched(wanted_second, second_factors)

    def low_rank_terms(rows, first_factors):
        return jnp.einsum(
            "bcj,bej->bce",
            rows.reshape(blocks, BLOCK, hidden_width),
            first_factors,
            preferred_element_type=f32,
        ).reshape(rows_local, -1)

    def adapter_delta(low_rank, second_factors):
        return jnp.einsum(
            "bcn,bnt->bct",
            low_rank.astype(bf16).reshape(blocks, BLOCK, -1),
            second_factors,
            preferred_element_type=f32,
        ).reshape(rows_local, slice_width).astype(bf16)

    hidden = (
        jax.nn.silu(gate_preactivation.astype(f32)) * up_preactivation.astype(f32)
    ).astype(bf16)
    if on_grid:
        base_part, delta = grid_sums(
            hidden, base_down_matrix, tensor_index, slice_width,
            lambda rows: low_rank_terms(rows, first_factors),
            lambda low_rank: adapter_delta(low_rank, second_factors),
        )
    else:
        delta = adapter_delta(lax.psum(low_rank_terms(hidden, first_factors), "tensor"), second_factors)
        base_part = lax.psum_scatter(
            jnp.dot(hidden, base_down_matrix, preferred_element_type=f32),
            "tensor",
            scatter_dimension=1,
            tiled=True,
        )
    combined = residual.astype(f32) + delta.astype(f32) + base_part
    layer_out = combined.astype(bf16)
    head = lax.dynamic_slice_in_dim(
        scoring_head_matrix, tensor_index * slice_width, slice_width
    )
    stats = jnp.stack([jnp.sum(combined * combined, 1), jnp.sum(combined * head[None, :], 1)])
    stats = stats.reshape(2 * blocks, BLOCK)
    stats = exchange_sum(stats, f32) if on_grid else lax.psum(stats, "tensor")
    square_sum, head_sum = stats[:blocks], stats[blocks:]
    scores = head_sum * lax.rsqrt(square_sum / model_width + EPSILON)
    position = jnp.arange(BLOCK, dtype=jnp.int32)
    inside = (position[None, :] >= block_span_start[:, None]) & (
        position[None, :] < block_span_end[:, None]
    )
    span_scores = jnp.sum(jnp.where(inside, scores, f32(0.0)), 1)
    return (layer_out, span_scores)


def solution(mesh):
    return jax.shard_map(
        shards,
        mesh=mesh,
        in_specs=(
            P(("groups", "dp"), "tensor"),
            P(("groups", "dp"), "tensor"),
            P("tensor", None),
            P("dp", "tensor", None),
            P("dp", None, "tensor"),
            P(("groups", "dp"), "tensor"),
            P(),
            P("groups"),
            P(("groups", "dp")),
            P(("groups", "dp")),
        ),
        out_specs=(P(("groups", "dp"), "tensor"), P(("groups", "dp"))),
        check_vma=False,
    )
```

```python
import jax
import jax.numpy as jnp
from jax import lax
from jax.experimental import pallas as pl
from jax.experimental.pallas import tpu as pltpu
from jax.sharding import PartitionSpec as P

BLOCK = 128
EPSILON = 1e-05

f32 = jnp.float32
bf16 = jnp.bfloat16

LINE = 4
PAIR = 2
ORDER = ((3, 2, 1, 0), (0, 3, 2, 1), (1, 0, 3, 2), (0, 1, 2, 3))
PIECES = 2
TILE = 512

ANYWHERE = pl.BlockSpec(memory_space=pl.ANY)
NO_COST = pl.CostEstimate(flops=0, bytes_accessed=0, transcendentals=0)


def along_line(value, hops):
    pairs = [(a * PAIR + y, b * PAIR + y) for a, b in hops for y in range(PAIR)]
    return lax.ppermute(value, "tensor", pairs)


def across(value, bit):
    size = LINE * PAIR
    return lax.ppermute(value, "tensor", [(t, t ^ bit) for t in range(size)])


def product_kernel(count, further, index_ref, rows_ref, weights_ref, *refs):
    result = jnp.dot(rows_ref[...], weights_ref[...], preferred_element_type=f32)
    size = result.shape[0] // count
    for n, ref in enumerate(refs[-count:]):
        ref[:size] = result[n * size : (n + 1) * size].astype(ref.dtype)
        if further:
            ref[size:] = refs[0][...].astype(ref.dtype)


def product(hidden, weights, tensor_index, turn, own, kind, width, earlier, piece, count, further=None):
    rows, depth = hidden.shape
    steps = width // TILE
    rows = rows if piece is None else rows // PIECES
    size = rows // count
    more = 0 if further is None else further.shape[0]

    def block(j, index):
        z, y = index[0] >> 1, index[0] & 1
        goal = ORDER[LINE - 1][turn]
        for other in range(LINE - 1):
            goal = jnp.where(z == other, ORDER[other][turn], goal)
        return (goal * PAIR + (y if own else 1 - y)) * steps + j

    return pl.pallas_call(
        lambda *refs: product_kernel(count, more, *refs),
        grid_spec=pltpu.PrefetchScalarGridSpec(
            num_scalar_prefetch=1,
            grid=(steps,),
            in_specs=[
                pl.BlockSpec((rows, depth), lambda j, index: (piece or 0, 0)),
                pl.BlockSpec((depth, TILE), lambda j, index: (0, block(j, index))),
            ]
            + [pl.BlockSpec((more, TILE), lambda j, index: (0, j))] * (more > 0)
            + [ANYWHERE] * len(earlier),
            out_specs=[pl.BlockSpec((size + more, TILE), lambda j, index: (0, j))] * count,
        ),
        out_shape=[pltpu.HBM((size + more, width), kind)] * count,
        compiler_params=pltpu.CompilerParams(vmem_limit_bytes=40 * 1024 * 1024),
        cost_estimate=NO_COST,
    )(tensor_index.reshape(1), hidden, weights, *([further] if more else []), *earlier)


def pick_kernel(ids_ref, *refs):
    refs[-1][...] = refs[0][...]


def pick(ids, factors, earlier=()):
    block = (1,) + factors.shape[1:]
    return pl.pallas_call(
        pick_kernel,
        grid_spec=pltpu.PrefetchScalarGridSpec(
            num_scalar_prefetch=1,
            grid=ids.shape,
            in_specs=[pl.BlockSpec(block, lambda n, ids: (ids[n], 0, 0))] + [ANYWHERE] * len(earlier),
            out_specs=pl.BlockSpec(block, lambda n, ids: (n, 0, 0)),
        ),
        out_shape=pltpu.HBM(ids.shape + factors.shape[1:], factors.dtype),
        cost_estimate=NO_COST,
    )(ids, factors, *earlier)


def exchange_sum(value, wire):
    for bit in (1, 2, 4):
        value = value + across(value.astype(wire), bit).astype(f32)
    return value


UP = ((0, 1), (1, 2), (2, 3))
DOWN = ((3, 2), (2, 1), (1, 0))


class Sequence:
    def __init__(self):
        self.last = None

    def __call__(self, stage, *values):
        if self.last is not None:
            values = lax.optimization_barrier((self.last,) + values)[1:]
        result = stage(*values)
        self.last = jax.tree.leaves(result)[0]
        return result


def grid_sums(hidden, weights, tensor_index, width, low_rank_terms):
    z = tensor_index >> 1
    low, last_z = z < LINE // 2, z == LINE - 1
    pieces = range(PIECES)
    then = Sequence()
    arrived, mine, first, second, third = {}, {}, {}, {}, {}
    add = lambda *terms: sum(t.astype(f32) for t in terms)
    narrow = lambda *terms: add(*terms).astype(bf16)
    size = hidden.shape[0] // PIECES

    def products(k, own, piece, count, further):
        kind = f32 if own else bf16
        out = then(
            lambda h, *more: product(h, weights, tensor_index, k, own, kind, width, (), piece, count, *more),
            hidden,
            *further,
        )
        for p, value in enumerate(out) if piece is None else [(piece, out[0])]:
            if own:
                mine[p, k] = value
            else:
                arrived[p, k] = across(value, 1)

    def theirs(k, *further, piece=None, count=PIECES):
        products(k, False, piece, 1 if piece is not None else count, further)

    def ours(k, piece=None, count=PIECES):
        products(k, True, piece, 1 if piece is not None else count, ())

    def sent(value, further):
        return value if further is None else jnp.concatenate([value, further.astype(bf16)], 0)

    def hop_1(p, further=None):
        value = sent(then(narrow, mine[p, 0], arrived[p, 0][:size]), further)
        first[p] = along_line(value, [UP[0], DOWN[0]])

    def hop_2(p, further=None):
        value = sent(then(narrow, mine[p, 1], arrived[p, 1], first[p][:size]), further)
        second[p] = (along_line(value, UP[:2]), along_line(value, DOWN[:2]))

    def hop_3(p, further):
        def stage(up, down, own, came_own, other, came_other):
            here, there = add(own, came_own), add(other, came_other)
            return narrow(here, up[:size]), narrow(jnp.where(last_z, here, there), down[:size])

        up, down = then(stage, *second[p], mine[p, 2], arrived[p, 2], mine[p, 0], arrived[p, 0][:size])
        third[p] = (along_line(sent(up, further), UP), along_line(sent(down, further), DOWN))

    wanted, low_rank_of = low_rank_terms(hidden)
    hidden = lax.optimization_barrier((wanted, hidden))[1]
    theirs(0, piece=0)
    low_rank, second_factors = low_rank_of()
    low_rank = low_rank.reshape(-1, width)
    theirs(0, low_rank, piece=1)
    ours(0)
    theirs(1, piece=0)
    hop_1(0)
    ours(1)
    theirs(1, piece=1)
    low_rank = add(low_rank, arrived[1, 0][size:])
    hop_1(1, low_rank)
    theirs(2, piece=0)
    ours(2)
    hop_2(0)
    theirs(2, piece=1)
    low_rank = add(low_rank, first[1][size:])
    hop_2(1, low_rank)
    theirs(3, count=1)
    ours(3, count=1)
    hop_3(0, None)
    up, down = second[1]
    low_rank = narrow(low_rank, jnp.where(low, down[size:], up[size:]))
    hop_3(1, low_rank)
    settled = then(add, *third[0])
    own_part = then(add, mine[0, 3], arrived[0, 3])
    up, down = third[1] = then(lambda *t: t, *third[1])
    low_rank = jnp.where(z == 0, down[size:], jnp.where(last_z, up[size:], low_rank))
    moved = jnp.concatenate([settled, add(up[:size], down[:size])], 0)
    base_part = own_part + moved
    return base_part, low_rank.reshape(hidden.shape[0], -1), second_factors


def shards(
    gate_preactivation,
    up_preactivation,
    base_down_matrix,
    adapter_first_factor,
    adapter_second_factor,
    residual,
    scoring_head_matrix,
    block_adapter_index,
    block_span_start,
    block_span_end,
):
    rows_local, hidden_width = gate_preactivation.shape
    slice_width = residual.shape[1]
    model_width = scoring_head_matrix.shape[0]
    blocks = rows_local // BLOCK
    adapters_here = adapter_first_factor.shape[0]
    data_index = lax.axis_index("dp")
    data_size = lax.axis_size("dp")
    tensor_index = lax.axis_index("tensor")
    on_grid = lax.axis_size("tensor") == LINE * PAIR

    ids = block_adapter_index.reshape(data_size, blocks)
    owner = lax.dynamic_index_in_dim(ids, data_index, 0, keepdims=False) // adapters_here
    first_turned = jnp.swapaxes(adapter_first_factor, 1, 2)
    steps = [step for step in range(1, data_size)] + [0]
    turned = jnp.concatenate(
        [lax.dynamic_slice_in_dim(ids, (data_index + step) % data_size, 1)[0] for step in steps]
    )
    turned = jnp.clip(turned - data_index * adapters_here, 0, adapters_here - 1)
    away = blocks * (data_size - 1)

    def low_rank_terms(rows):
        wanted_first = pick(turned[:away], first_turned)

        def terms(*earlier):
            wanted_second = pick(turned[:away], adapter_second_factor, earlier)
            first_factors = pick(turned[away:], first_turned, earlier)
            second_factors = pick(turned[away:], adapter_second_factor, earlier)
            for n, step in enumerate(steps[:-1]):
                hop = [(d, (d + step) % data_size) for d in range(data_size)]
                take = (owner == (data_index - step) % data_size)[:, None, None]

                def fetched(wanted, kept):
                    came = lax.ppermute(wanted[n * blocks : (n + 1) * blocks], "dp", hop)
                    return jnp.where(take, came, kept)

                first_factors = fetched(wanted_first, first_factors)
                second_factors = fetched(wanted_second, second_factors)
            product = jnp.einsum(
                "bcj,bej->bce",
                rows.reshape(blocks, BLOCK, hidden_width),
                first_factors,
                preferred_element_type=f32,
            ).reshape(rows_local, -1)
            return product, second_factors

        return wanted_first, terms

    def adapter_delta(low_rank, second_factors):
        return jnp.einsum(
            "bcn,bnt->bct",
            low_rank.astype(bf16).reshape(blocks, BLOCK, -1),
            second_factors,
            preferred_element_type=f32,
        ).reshape(rows_local, slice_width).astype(bf16)

    hidden = (
        jax.nn.silu(gate_preactivation.astype(f32)) * up_preactivation.astype(f32)
    ).astype(bf16)
    if on_grid:
        base_part, low_rank, second_factors = grid_sums(
            hidden, base_down_matrix, tensor_index, slice_width, low_rank_terms
        )
        delta = adapter_delta(low_rank, second_factors)
    else:
        low_rank, second_factors = low_rank_terms(hidden)[1]()
        delta = adapter_delta(lax.psum(low_rank, "tensor"), second_factors)
        base_part = lax.psum_scatter(
            jnp.dot(hidden, base_down_matrix, preferred_element_type=f32),
            "tensor",
            scatter_dimension=1,
            tiled=True,
        )
    combined = residual.astype(f32) + delta.astype(f32) + base_part
    layer_out = combined.astype(bf16)
    head = lax.dynamic_slice_in_dim(
        scoring_head_matrix, tensor_index * slice_width, slice_width
    )
    stats = jnp.stack([jnp.sum(combined * combined, 1), jnp.sum(combined * head[None, :], 1)])
    stats = stats.reshape(2 * blocks, BLOCK)
    stats = exchange_sum(stats, f32) if on_grid else lax.psum(stats, "tensor")
    square_sum, head_sum = stats[:blocks], stats[blocks:]
    scores = head_sum * lax.rsqrt(square_sum / model_width + EPSILON)
    position = jnp.arange(BLOCK, dtype=jnp.int32)
    inside = (position[None, :] >= block_span_start[:, None]) & (
        position[None, :] < block_span_end[:, None]
    )
    span_scores = jnp.sum(jnp.where(inside, scores, f32(0.0)), 1)
    return (layer_out, span_scores)


def solution(mesh):
    return jax.shard_map(
        shards,
        mesh=mesh,
        in_specs=(
            P(("groups", "dp"), "tensor"),
            P(("groups", "dp"), "tensor"),
            P("tensor", None),
            P("dp", "tensor", None),
            P("dp", None, "tensor"),
            P(("groups", "dp"), "tensor"),
            P(),
            P("groups"),
            P(("groups", "dp")),
            P(("groups", "dp")),
        ),
        out_specs=(P(("groups", "dp"), "tensor"), P(("groups", "dp"))),
        check_vma=False,
    )
```

```python
import jax
import jax.numpy as jnp
from jax import lax
from jax.experimental import pallas as pl
from jax.experimental.pallas import tpu as pltpu
from jax.sharding import PartitionSpec as P

BLOCK = 128
EPSILON = 1e-05

f32 = jnp.float32
bf16 = jnp.bfloat16

LINE = 4
PAIR = 2
ORDER = ((3, 2, 1, 0), (0, 3, 2, 1), (1, 0, 3, 2), (0, 1, 2, 3))
PIECES = 2
TILE = 512

ANYWHERE = pl.BlockSpec(memory_space=pl.ANY)
NO_COST = pl.CostEstimate(flops=0, bytes_accessed=0, transcendentals=0)


def along_line(value, hops):
    pairs = [(a * PAIR + y, b * PAIR + y) for a, b in hops for y in range(PAIR)]
    return lax.ppermute(value, "tensor", pairs)


def across(value, bit):
    size = LINE * PAIR
    return lax.ppermute(value, "tensor", [(t, t ^ bit) for t in range(size)])


def product_kernel(count, index_ref, rows_ref, weights_ref, *refs):
    result = jnp.dot(rows_ref[...], weights_ref[...], preferred_element_type=f32)
    size = result.shape[0] // count
    for n, ref in enumerate(refs[-count:]):
        ref[...] = result[n * size : (n + 1) * size].astype(ref.dtype)


def product(hidden, weights, tensor_index, turn, own, kind, width, piece, count):
    rows, depth = hidden.shape
    steps = width // TILE
    rows = rows if piece is None else rows // PIECES
    size = rows // count

    def block(j, index):
        z, y = index[0] >> 1, index[0] & 1
        goal = ORDER[LINE - 1][turn]
        for other in range(LINE - 1):
            goal = jnp.where(z == other, ORDER[other][turn], goal)
        return (goal * PAIR + (y if own else 1 - y)) * steps + j

    return pl.pallas_call(
        lambda *refs: product_kernel(count, *refs),
        grid_spec=pltpu.PrefetchScalarGridSpec(
            num_scalar_prefetch=1,
            grid=(steps,),
            in_specs=[
                pl.BlockSpec((rows, depth), lambda j, index: (piece or 0, 0)),
                pl.BlockSpec((depth, TILE), lambda j, index: (0, block(j, index))),
            ],
            out_specs=[pl.BlockSpec((size, TILE), lambda j, index: (0, j))] * count,
        ),
        out_shape=[pltpu.HBM((size, width), kind)] * count,
        compiler_params=pltpu.CompilerParams(vmem_limit_bytes=40 * 1024 * 1024),
        cost_estimate=NO_COST,
    )(tensor_index.reshape(1), hidden, weights)


def pick_kernel(ids_ref, *refs):
    count = len(refs) // 2
    for n in range(count):
        refs[n - count][...] = refs[n][...]


def pick(ids, factors, sets, earlier=()):
    block = (1,) + factors.shape[1:]
    count = ids.shape[0] // sets
    spec = lambda s: pl.BlockSpec(block, lambda n, ids: (ids[s * count + n], 0, 0))
    return pl.pallas_call(
        pick_kernel,
        grid_spec=pltpu.PrefetchScalarGridSpec(
            num_scalar_prefetch=1,
            grid=(count,),
            in_specs=[spec(s) for s in range(sets)] + [ANYWHERE] * len(earlier),
            out_specs=[pl.BlockSpec(block, lambda n, ids: (n, 0, 0))] * sets,
        ),
        out_shape=[pltpu.HBM((count,) + factors.shape[1:], factors.dtype)] * sets,
        cost_estimate=NO_COST,
    )(ids, *[factors] * sets, *earlier)


def exchange_sum(value):
    a, b, c = [across(value, bit) for bit in (1, 2, 3)]
    value = (value + a) + (b + c)
    return value + across(value, 4)


UP = ((0, 1), (1, 2), (2, 3))
DOWN = ((3, 2), (2, 1), (1, 0))


class Sequence:
    def __init__(self):
        self.last = None

    def __call__(self, stage, *values):
        if self.last is not None:
            values = lax.optimization_barrier((self.last,) + values)[1:]
        result = stage(*values)
        self.last = jax.tree.leaves(result)[0]
        return result


def grid_sums(hidden, weights, residual, tensor_index, low_rank_terms, adapter_delta):
    width = residual.shape[1]
    z = tensor_index >> 1
    low, last_z = z < LINE // 2, z == LINE - 1
    then = Sequence()
    arrived, mine, first, second, third = {}, {}, {}, {}, {}
    add = lambda *terms: sum(t.astype(f32) for t in terms)
    narrow = lambda *terms: add(*terms).astype(bf16)
    size = hidden.shape[0] // PIECES

    def products(k, own, piece, count):
        kind = f32 if own else bf16
        return then(
            lambda h: product(h, weights, tensor_index, k, own, kind, width, piece, count), hidden
        )

    def theirs(k, piece=0, whole=False):
        value = products(k, False, None if whole else piece, 1)[0]
        arrived[piece, k] = across(value, 1)

    def ours(k):
        for p, value in enumerate(products(k, True, None, PIECES)):
            mine[p, k] = value

    def sent(value, further):
        return value if further is None else jnp.concatenate([value, further.astype(bf16)], 0)

    def hop_1(p, further=None):
        value = sent(then(narrow, mine[p, 0], arrived[p, 0][:size]), further)
        first[p] = along_line(value, [UP[0], DOWN[0]])

    def hop_2(p, further=None):
        value = sent(then(narrow, mine[p, 1], arrived[p, 1], first[p][:size]), further)
        second[p] = (along_line(value, UP[:2]), along_line(value, DOWN[:2]))

    def hop_3(p, further):
        def stage(up, down, own, came_own, other, came_other):
            here, there = add(own, came_own), add(other, came_other)
            return narrow(here, up[:size]), narrow(jnp.where(last_z, here, there), down[:size])

        up, down = then(stage, *second[p], mine[p, 2], arrived[p, 2], mine[p, 0], arrived[p, 0][:size])
        third[p] = (along_line(sent(up, further), UP), along_line(sent(down, further), DOWN))

    theirs(0, 0)
    low_rank_of, second_factors_of = low_rank_terms(then.last)
    value = products(0, False, 1, 1)[0]
    low_rank = low_rank_of(hidden).reshape(-1, width)
    arrived[1, 0] = across(then(sent, value, low_rank), 1)
    ours(0)
    theirs(1, 0)
    hop_1(0)
    ours(1)
    theirs(1, 1)
    low_rank = add(low_rank, arrived[1, 0][size:])
    hop_1(1, low_rank)
    theirs(2, 0)
    ours(2)
    hop_2(0)
    theirs(2, 1)
    low_rank = add(low_rank, first[1][size:])
    hop_2(1, low_rank)
    hop_3(0, None)
    theirs(3, whole=True)
    ours(3)
    up, down = second[1]
    low_rank = narrow(low_rank, jnp.where(low, down[size:], up[size:]))
    hop_3(1, low_rank)
    second_factors = second_factors_of(mine[0, 3])
    settled = then(add, *third[0], mine[0, 3], residual[:size])
    up, down = third[1] = then(lambda *t: t, *third[1])
    low_rank = jnp.where(z == 0, down[size:], jnp.where(last_z, up[size:], low_rank))
    delta = adapter_delta(low_rank.reshape(hidden.shape[0], -1), second_factors)

    def stage(settled, up, down, own, kept, delta):
        return jnp.concatenate([settled, add(up[:size], down[:size], own, kept)], 0) + delta.astype(f32)

    settled = then(stage, settled, up, down, mine[1, 3], residual[size:], delta)
    return add(*lax.optimization_barrier((settled, arrived[0, 3])))


def shards(
    gate_preactivation,
    up_preactivation,
    base_down_matrix,
    adapter_first_factor,
    adapter_second_factor,
    residual,
    scoring_head_matrix,
    block_adapter_index,
    block_span_start,
    block_span_end,
):
    rows_local, hidden_width = gate_preactivation.shape
    slice_width = residual.shape[1]
    model_width = scoring_head_matrix.shape[0]
    blocks = rows_local // BLOCK
    adapters_here = adapter_first_factor.shape[0]
    data_index = lax.axis_index("dp")
    data_size = lax.axis_size("dp")
    tensor_index = lax.axis_index("tensor")
    on_grid = lax.axis_size("tensor") == LINE * PAIR

    ids = block_adapter_index.reshape(data_size, blocks)
    owner = lax.dynamic_index_in_dim(ids, data_index, 0, keepdims=False) // adapters_here
    first_turned = jnp.swapaxes(adapter_first_factor, 1, 2)
    steps = [step for step in range(1, data_size)] + [0]
    turned = jnp.concatenate(
        [lax.dynamic_slice_in_dim(ids, (data_index + step) % data_size, 1)[0] for step in steps]
    )
    turned = jnp.clip(turned - data_index * adapters_here, 0, adapters_here - 1)

    def fetched(factors, earlier):
        *wanted, kept = pick(turned, factors, data_size, earlier)
        for n, step in enumerate(steps[:-1]):
            hop = [(d, (d + step) % data_size) for d in range(data_size)]
            take = (owner == (data_index - step) % data_size)[:, None, None]
            kept = jnp.where(take, lax.ppermute(wanted[n], "dp", hop), kept)
        return kept

    def low_rank_terms(*earlier):
        first_factors = fetched(first_turned, earlier)

        def terms(rows):
            return jnp.einsum(
                "bcj,bej->bce",
                rows.reshape(blocks, BLOCK, hidden_width),
                first_factors,
                preferred_element_type=f32,
            ).reshape(rows_local, -1)

        return terms, lambda *earlier: fetched(adapter_second_factor, earlier)

    def adapter_delta(low_rank, second_factors):
        return jnp.einsum(
            "bcn,bnt->bct",
            low_rank.astype(bf16).reshape(blocks, BLOCK, -1),
            second_factors,
            preferred_element_type=f32,
        ).reshape(rows_local, slice_width).astype(bf16)

    hidden = (
        jax.nn.silu(gate_preactivation.astype(f32)) * up_preactivation.astype(f32)
    ).astype(bf16)
    if on_grid:
        combined = grid_sums(
            hidden, base_down_matrix, residual, tensor_index, low_rank_terms, adapter_delta
        )
    else:
        low_rank_of, second_factors_of = low_rank_terms()
        delta = adapter_delta(lax.psum(low_rank_of(hidden), "tensor"), second_factors_of())
        base_part = lax.psum_scatter(
            jnp.dot(hidden, base_down_matrix, preferred_element_type=f32),
            "tensor",
            scatter_dimension=1,
            tiled=True,
        )
        combined = residual.astype(f32) + delta.astype(f32) + base_part
    layer_out = combined.astype(bf16)
    head = lax.dynamic_slice_in_dim(
        scoring_head_matrix, tensor_index * slice_width, slice_width
    )
    stats = jnp.stack([jnp.sum(combined * combined, 1), jnp.sum(combined * head[None, :], 1)])
    stats = stats.reshape(2 * blocks, BLOCK)
    stats = exchange_sum(stats) if on_grid else lax.psum(stats, "tensor")
    square_sum, head_sum = stats[:blocks], stats[blocks:]
    scores = head_sum * lax.rsqrt(square_sum / model_width + EPSILON)
    position = jnp.arange(BLOCK, dtype=jnp.int32)
    inside = (position[None, :] >= block_span_start[:, None]) & (
        position[None, :] < block_span_end[:, None]
    )
    span_scores = jnp.sum(jnp.where(inside, scores, f32(0.0)), 1)
    return (layer_out, span_scores)


def solution(mesh):
    return jax.shard_map(
        shards,
        mesh=mesh,
        in_specs=(
            P(("groups", "dp"), "tensor"),
            P(("groups", "dp"), "tensor"),
            P("tensor", None),
            P("dp", "tensor", None),
            P("dp", None, "tensor"),
            P(("groups", "dp"), "tensor"),
            P(),
            P("groups"),
            P(("groups", "dp")),
            P(("groups", "dp")),
        ),
        out_specs=(P(("groups", "dp"), "tensor"), P(("groups", "dp"))),
        check_vma=False,
    )
```

```python
import jax
import jax.numpy as jnp
from jax import lax
from jax.experimental import pallas as pl
from jax.experimental.pallas import tpu as pltpu
from jax.sharding import PartitionSpec as P

BLOCK = 128
EPSILON = 1e-05

f32 = jnp.float32
bf16 = jnp.bfloat16

LINE = 4
PAIR = 2
ORDER = ((3, 2, 1, 0), (0, 3, 2, 1), (1, 0, 3, 2), (0, 1, 2, 3))
PIECES = 2
TILE = 512

ANYWHERE = pl.BlockSpec(memory_space=pl.ANY)
NO_COST = pl.CostEstimate(flops=0, bytes_accessed=0, transcendentals=0)


def along_line(value, hops):
    pairs = [(a * PAIR + y, b * PAIR + y) for a, b in hops for y in range(PAIR)]
    return lax.ppermute(value, "tensor", pairs)


def across(value, bit):
    size = LINE * PAIR
    return lax.ppermute(value, "tensor", [(t, t ^ bit) for t in range(size)])


def product_kernel(inputs, count, further, index_ref, weights_ref, *refs):
    outs = refs[-count:]
    for n, rows_ref in enumerate(refs[:inputs]):
        result = jnp.dot(rows_ref[...], weights_ref[...], preferred_element_type=f32)
        size = result.shape[0]
        at = 0 if count == inputs else n * size
        ref = outs[n if count == inputs else 0]
        ref[at : at + size] = result.astype(ref.dtype)
        if further:
            ref[size:] = refs[inputs][...].astype(ref.dtype)


def product(hidden, weights, tensor_index, turn, own, kind, width, earlier, piece, count, further=None):
    inputs = hidden if piece is None else hidden[piece : piece + 1]
    rows, depth = inputs[0].shape
    steps = width // TILE
    size = rows * len(inputs) // count
    more = 0 if further is None else further.shape[0]

    def block(j, index):
        z, y = index[0] >> 1, index[0] & 1
        goal = ORDER[LINE - 1][turn]
        for other in range(LINE - 1):
            goal = jnp.where(z == other, ORDER[other][turn], goal)
        return (goal * PAIR + (y if own else 1 - y)) * steps + j

    return pl.pallas_call(
        lambda *refs: product_kernel(len(inputs), count, more, *refs),
        grid_spec=pltpu.PrefetchScalarGridSpec(
            num_scalar_prefetch=1,
            grid=(steps,),
            in_specs=[
                pl.BlockSpec((depth, TILE), lambda j, index: (0, block(j, index))),
            ]
            + [pl.BlockSpec((rows, depth), lambda j, index: (0, 0))] * len(inputs)
            + [pl.BlockSpec((more, TILE), lambda j, index: (0, j))] * (more > 0)
            + [ANYWHERE] * len(earlier),
            out_specs=[pl.BlockSpec((size + more, TILE), lambda j, index: (0, j))] * count,
        ),
        out_shape=[pltpu.HBM((size + more, width), kind)] * count,
        compiler_params=pltpu.CompilerParams(vmem_limit_bytes=40 * 1024 * 1024),
        cost_estimate=NO_COST,
    )(tensor_index.reshape(1), weights, *inputs, *([further] if more else []), *earlier)


def pick_kernel(ids_ref, factors_ref, *refs):
    out_ref, semaphores = refs[-2:]
    copies = [
        pltpu.make_async_copy(factors_ref.at[ids_ref[n]], out_ref.at[n], semaphores.at[n])
        for n in range(out_ref.shape[0])
    ]
    for copy in copies:
        copy.start()
    for copy in copies:
        copy.wait()


def pick(ids, factors, earlier=()):
    shape = ids.shape + factors.shape[1:]
    return pl.pallas_call(
        pick_kernel,
        grid_spec=pltpu.PrefetchScalarGridSpec(
            num_scalar_prefetch=1,
            grid=(1,),
            in_specs=[pl.BlockSpec(memory_space=pltpu.HBM)] + [ANYWHERE] * len(earlier),
            out_specs=pl.BlockSpec(shape, lambda i, ids: (0, 0, 0)),
            scratch_shapes=[pltpu.SemaphoreType.DMA(ids.shape)],
        ),
        out_shape=pltpu.HBM(shape, factors.dtype),
        compiler_params=pltpu.CompilerParams(vmem_limit_bytes=60 * 1024 * 1024),
        cost_estimate=NO_COST,
    )(ids, factors, *earlier)


def exchange_sum(value, wire):
    for bit in (1, 2, 4):
        value = value + across(value.astype(wire), bit).astype(f32)
    return value


UP = ((0, 1), (1, 2), (2, 3))
DOWN = ((3, 2), (2, 1), (1, 0))


class Sequence:
    def __init__(self):
        self.last = None

    def __call__(self, stage, *values):
        if self.last is not None:
            values = lax.optimization_barrier((self.last,) + values)[1:]
        result = stage(*values)
        self.last = jax.tree.leaves(result)[0]
        return result


def grid_sums(hidden, weights, tensor_index, width, low_rank_terms):
    z = tensor_index >> 1
    low, last_z = z < LINE // 2, z == LINE - 1
    pieces = range(PIECES)
    then = Sequence()
    arrived, mine, first, second, third = {}, {}, {}, {}, {}
    add = lambda *terms: sum(t.astype(f32) for t in terms)
    narrow = lambda *terms: add(*terms).astype(bf16)
    size = hidden[0].shape[0]

    def products(k, own, piece, count, further):
        kind = f32 if own else bf16
        out = then(
            lambda w, *more: product(hidden, w, tensor_index, k, own, kind, width, (), piece, count, *more),
            weights,
            *further,
        )
        for p, value in enumerate(out) if piece is None else [(piece, out[0])]:
            if own:
                mine[p, k] = value
            else:
                arrived[p, k] = across(value, 1)

    def theirs(k, *further, piece=None, count=PIECES):
        products(k, False, piece, 1 if piece is not None else count, further)

    def ours(k, piece=None, count=PIECES):
        products(k, True, piece, 1 if piece is not None else count, ())

    def sent(value, further):
        return value if further is None else jnp.concatenate([value, further.astype(bf16)], 0)

    def hop_1(p, further=None):
        value = sent(then(narrow, mine[p, 0], arrived[p, 0][:size]), further)
        first[p] = along_line(value, [UP[0], DOWN[0]])

    def hop_2(p, further=None):
        value = sent(then(narrow, mine[p, 1], arrived[p, 1], first[p][:size]), further)
        second[p] = (along_line(value, UP[:2]), along_line(value, DOWN[:2]))

    def hop_3(p, further):
        def stage(up, down, own, came_own, other, came_other):
            here, there = add(own, came_own), add(other, came_other)
            return narrow(here, up[:size]), narrow(jnp.where(last_z, here, there), down[:size])

        up, down = then(stage, *second[p], mine[p, 2], arrived[p, 2], mine[p, 0], arrived[p, 0][:size])
        third[p] = (along_line(sent(up, further), UP), along_line(sent(down, further), DOWN))

    wanted, low_rank_of = low_rank_terms(hidden)
    hidden[0] = lax.optimization_barrier((wanted, hidden[0]))[1]
    theirs(0, piece=0)
    low_rank, second_factors = low_rank_of()
    low_rank = low_rank.reshape(-1, width)
    theirs(0, low_rank, piece=1)
    ours(0)
    theirs(1, piece=0)
    hop_1(0)
    ours(1)
    theirs(1, piece=1)
    low_rank = add(low_rank, arrived[1, 0][size:])
    hop_1(1, low_rank)
    theirs(2, piece=0)
    ours(2)
    hop_2(0)
    theirs(2, piece=1)
    low_rank = add(low_rank, first[1][size:])
    hop_2(1, low_rank)
    theirs(3, count=1)
    ours(3, count=1)
    hop_3(0, None)
    up, down = second[1]
    low_rank = narrow(low_rank, jnp.where(low, down[size:], up[size:]))
    hop_3(1, low_rank)
    settled = then(add, *third[0])
    own_part = then(add, mine[0, 3], arrived[0, 3])
    up, down = third[1] = then(lambda *t: t, *third[1])
    low_rank = jnp.where(z == 0, down[size:], jnp.where(last_z, up[size:], low_rank))
    moved = jnp.concatenate([settled, add(up[:size], down[:size])], 0)
    base_part = own_part + moved
    return base_part, low_rank.reshape(PIECES * size, -1), second_factors


def shards(
    gate_preactivation,
    up_preactivation,
    base_down_matrix,
    adapter_first_factor,
    adapter_second_factor,
    residual,
    scoring_head_matrix,
    block_adapter_index,
    block_span_start,
    block_span_end,
):
    rows_local, hidden_width = gate_preactivation.shape
    slice_width = residual.shape[1]
    model_width = scoring_head_matrix.shape[0]
    blocks = rows_local // BLOCK
    adapters_here = adapter_first_factor.shape[0]
    data_index = lax.axis_index("dp")
    data_size = lax.axis_size("dp")
    tensor_index = lax.axis_index("tensor")
    on_grid = lax.axis_size("tensor") == LINE * PAIR

    ids = block_adapter_index.reshape(data_size, blocks)
    owner = lax.dynamic_index_in_dim(ids, data_index, 0, keepdims=False) // adapters_here
    first_turned = jnp.swapaxes(adapter_first_factor, 1, 2)
    steps = [step for step in range(1, data_size)] + [0]
    turned = jnp.concatenate(
        [lax.dynamic_slice_in_dim(ids, (data_index + step) % data_size, 1)[0] for step in steps]
    )
    turned = jnp.clip(turned - data_index * adapters_here, 0, adapters_here - 1)
    away = blocks * (data_size - 1)

    def low_rank_terms(rows):
        wanted_first = pick(turned[:away], first_turned)

        def terms(*earlier):
            wanted_second = pick(turned[:away], adapter_second_factor, earlier)
            first_factors = pick(turned[away:], first_turned, earlier)
            second_factors = pick(turned[away:], adapter_second_factor, earlier)
            for n, step in enumerate(steps[:-1]):
                hop = [(d, (d + step) % data_size) for d in range(data_size)]
                take = (owner == (data_index - step) % data_size)[:, None, None]

                def fetched(wanted, kept):
                    came = lax.ppermute(wanted[n * blocks : (n + 1) * blocks], "dp", hop)
                    return jnp.where(take, came, kept)

                first_factors = fetched(wanted_first, first_factors)
                second_factors = fetched(wanted_second, second_factors)
            each = blocks // len(rows)
            product = [
                jnp.einsum(
                    "bcj,bej->bce",
                    part.reshape(each, BLOCK, hidden_width),
                    first_factors[n * each : (n + 1) * each],
                    preferred_element_type=f32,
                ).reshape(each * BLOCK, -1)
                for n, part in enumerate(rows)
            ]
            return jnp.concatenate(product, 0), second_factors

        return wanted_first, terms

    def adapter_delta(low_rank, second_factors):
        return jnp.einsum(
            "bcn,bnt->bct",
            low_rank.astype(bf16).reshape(blocks, BLOCK, -1),
            second_factors,
            preferred_element_type=f32,
        ).reshape(rows_local, slice_width).astype(bf16)

    def hidden_of(gate, up):
        return (jax.nn.silu(gate.astype(f32)) * up.astype(f32)).astype(bf16)

    if on_grid:
        half = rows_local // PIECES
        hidden = [
            hidden_of(gate_preactivation[n * half : (n + 1) * half], up_preactivation[n * half : (n + 1) * half])
            for n in range(PIECES)
        ]
        base_part, low_rank, second_factors = grid_sums(
            hidden, base_down_matrix, tensor_index, slice_width, low_rank_terms
        )
        delta = adapter_delta(low_rank, second_factors)
    else:
        hidden = hidden_of(gate_preactivation, up_preactivation)
        low_rank, second_factors = low_rank_terms([hidden])[1]()
        delta = adapter_delta(lax.psum(low_rank, "tensor"), second_factors)
        base_part = lax.psum_scatter(
            jnp.dot(hidden, base_down_matrix, preferred_element_type=f32),
            "tensor",
            scatter_dimension=1,
            tiled=True,
        )
    combined = residual.astype(f32) + delta.astype(f32) + base_part
    layer_out = combined.astype(bf16)
    head = lax.dynamic_slice_in_dim(
        scoring_head_matrix, tensor_index * slice_width, slice_width
    )
    stats = jnp.stack([jnp.sum(combined * combined, 1), jnp.sum(combined * head[None, :], 1)])
    stats = stats.reshape(2 * blocks, BLOCK)
    stats = exchange_sum(stats, f32) if on_grid else lax.psum(stats, "tensor")
    square_sum, head_sum = stats[:blocks], stats[blocks:]
    scores = head_sum * lax.rsqrt(square_sum / model_width + EPSILON)
    position = jnp.arange(BLOCK, dtype=jnp.int32)
    inside = (position[None, :] >= block_span_start[:, None]) & (
        position[None, :] < block_span_end[:, None]
    )
    span_scores = jnp.sum(jnp.where(inside, scores, f32(0.0)), 1)
    return (layer_out, span_scores)


def solution(mesh):
    return jax.shard_map(
        shards,
        mesh=mesh,
        in_specs=(
            P(("groups", "dp"), "tensor"),
            P(("groups", "dp"), "tensor"),
            P("tensor", None),
            P("dp", "tensor", None),
            P("dp", None, "tensor"),
            P(("groups", "dp"), "tensor"),
            P(),
            P("groups"),
            P(("groups", "dp")),
            P(("groups", "dp")),
        ),
        out_specs=(P(("groups", "dp"), "tensor"), P(("groups", "dp"))),
        check_vma=False,
    )
```

```python
import jax
import jax.numpy as jnp
from jax import lax
from jax.experimental import pallas as pl
from jax.experimental.pallas import tpu as pltpu
from jax.sharding import PartitionSpec as P

BLOCK = 128
EPSILON = 1e-05

f32 = jnp.float32
bf16 = jnp.bfloat16

LINE = 4
PAIR = 2
ORDER = ((3, 2, 1, 0), (0, 3, 2, 1), (1, 0, 3, 2), (0, 1, 2, 3))
PIECES = 2
TILE = 512

ANYWHERE = pl.BlockSpec(memory_space=pl.ANY)
NO_COST = pl.CostEstimate(flops=0, bytes_accessed=0, transcendentals=0)


def along_line(value, hops):
    pairs = [(a * PAIR + y, b * PAIR + y) for a, b in hops for y in range(PAIR)]
    return lax.ppermute(value, "tensor", pairs)


def across(value, bit):
    size = LINE * PAIR
    return lax.ppermute(value, "tensor", [(t, t ^ bit) for t in range(size)])


def product_kernel(inputs, count, further, index_ref, weights_ref, *refs):
    outs = refs[-count:]
    for n, rows_ref in enumerate(refs[:inputs]):
        result = jnp.dot(rows_ref[...], weights_ref[...], preferred_element_type=f32)
        size = result.shape[0]
        at = 0 if count == inputs else n * size
        ref = outs[n if count == inputs else 0]
        ref[at : at + size] = result.astype(ref.dtype)
        if further:
            ref[size:] = refs[inputs][...].astype(ref.dtype)


def product(hidden, weights, tensor_index, turn, own, kind, width, earlier, piece, count, further=None):
    inputs = hidden if piece is None else hidden[piece : piece + 1]
    rows, depth = inputs[0].shape
    steps = width // TILE
    size = rows * len(inputs) // count
    more = 0 if further is None else further.shape[0]

    def block(j, index):
        z, y = index[0] >> 1, index[0] & 1
        goal = ORDER[LINE - 1][turn]
        for other in range(LINE - 1):
            goal = jnp.where(z == other, ORDER[other][turn], goal)
        return (goal * PAIR + (y if own else 1 - y)) * steps + j

    return pl.pallas_call(
        lambda *refs: product_kernel(len(inputs), count, more, *refs),
        grid_spec=pltpu.PrefetchScalarGridSpec(
            num_scalar_prefetch=1,
            grid=(steps,),
            in_specs=[
                pl.BlockSpec((depth, TILE), lambda j, index: (0, block(j, index))),
            ]
            + [pl.BlockSpec((rows, depth), lambda j, index: (0, 0))] * len(inputs)
            + [pl.BlockSpec((more, TILE), lambda j, index: (0, j))] * (more > 0)
            + [ANYWHERE] * len(earlier),
            out_specs=[pl.BlockSpec((size + more, TILE), lambda j, index: (0, j))] * count,
        ),
        out_shape=[pltpu.HBM((size + more, width), kind)] * count,
        compiler_params=pltpu.CompilerParams(vmem_limit_bytes=40 * 1024 * 1024),
        cost_estimate=NO_COST,
    )(tensor_index.reshape(1), weights, *inputs, *([further] if more else []), *earlier)


def pick_kernel(ids_ref, factors_ref, *refs):
    out_ref, held_ref, came, left = refs[-4:]
    places = range(out_ref.shape[0])
    into = [pltpu.make_async_copy(factors_ref.at[ids_ref[n]], held_ref.at[n], came.at[n]) for n in places]
    out = [pltpu.make_async_copy(held_ref.at[n], out_ref.at[n], left.at[n]) for n in places]
    for n in places:
        into[n].start()
    for n in places:
        into[n].wait()
        out[n].start()
    for n in places:
        out[n].wait()


def pick(ids, factors, earlier=()):
    shape = ids.shape + factors.shape[1:]
    return pl.pallas_call(
        pick_kernel,
        grid_spec=pltpu.PrefetchScalarGridSpec(
            num_scalar_prefetch=1,
            grid=(1,),
            in_specs=[pl.BlockSpec(memory_space=pltpu.HBM)] + [ANYWHERE] * len(earlier),
            out_specs=pl.BlockSpec(memory_space=pltpu.HBM),
            scratch_shapes=[pltpu.VMEM(shape, factors.dtype)] + [pltpu.SemaphoreType.DMA(ids.shape)] * 2,
        ),
        out_shape=pltpu.HBM(shape, factors.dtype),
        compiler_params=pltpu.CompilerParams(vmem_limit_bytes=60 * 1024 * 1024),
        cost_estimate=NO_COST,
    )(ids, factors, *earlier)


def exchange_sum(value, wire):
    for bit in (4, 2, 1):
        value = value + across(value.astype(wire), bit).astype(f32)
    return value


UP = ((0, 1), (1, 2), (2, 3))
DOWN = ((3, 2), (2, 1), (1, 0))


class Sequence:
    def __init__(self):
        self.last = None

    def __call__(self, stage, *values):
        if self.last is not None:
            values = lax.optimization_barrier((self.last,) + values)[1:]
        result = stage(*values)
        self.last = jax.tree.leaves(result)[0]
        return result


def grid_sums(hidden, weights, tensor_index, width, low_rank_terms):
    z = tensor_index >> 1
    low, last_z = z < LINE // 2, z == LINE - 1
    pieces = range(PIECES)
    then = Sequence()
    arrived, mine, first, second, third = {}, {}, {}, {}, {}
    add = lambda *terms: sum(t.astype(f32) for t in terms)
    narrow = lambda *terms: add(*terms).astype(bf16)
    size = hidden[0].shape[0]

    def products(k, own, piece, count, further):
        kind = f32 if own else bf16
        out = then(
            lambda w, *more: product(hidden, w, tensor_index, k, own, kind, width, (), piece, count, *more),
            weights,
            *further,
        )
        for p, value in enumerate(out) if piece is None else [(piece, out[0])]:
            if own:
                mine[p, k] = value
            else:
                arrived[p, k] = across(value, 1)

    def theirs(k, *further, piece=None, count=PIECES):
        products(k, False, piece, 1 if piece is not None else count, further)

    def ours(k, piece=None, count=PIECES):
        products(k, True, piece, 1 if piece is not None else count, ())

    def sent(value, further):
        return value if further is None else jnp.concatenate([value, further.astype(bf16)], 0)

    def hop_1(p, further=None):
        value = sent(then(narrow, mine[p, 0], arrived[p, 0][:size]), further)
        first[p] = along_line(value, [UP[0], DOWN[0]])

    def hop_2(p, further=None):
        value = sent(then(narrow, mine[p, 1], arrived[p, 1], first[p][:size]), further)
        second[p] = (along_line(value, UP[:2]), along_line(value, DOWN[:2]))

    def hop_3(p, further):
        def stage(up, down, own, came_own, other, came_other):
            here, there = add(own, came_own), add(other, came_other)
            return narrow(here, up[:size]), narrow(jnp.where(last_z, here, there), down[:size])

        up, down = then(stage, *second[p], mine[p, 2], arrived[p, 2], mine[p, 0], arrived[p, 0][:size])
        third[p] = (along_line(sent(up, further), UP), along_line(sent(down, further), DOWN))

    wanted, low_rank_of = low_rank_terms(hidden)
    hidden[0] = lax.optimization_barrier((wanted, hidden[0]))[1]
    theirs(0, piece=0)
    low_rank, second_factors = low_rank_of()
    low_rank = low_rank.reshape(-1, width)
    theirs(0, low_rank, piece=1)
    ours(0)
    theirs(1, piece=0)
    hop_1(0)
    ours(1)
    theirs(1, piece=1)
    low_rank = add(low_rank, arrived[1, 0][size:])
    hop_1(1, low_rank)
    theirs(2, piece=0)
    ours(2)
    hop_2(0)
    theirs(2, piece=1)
    low_rank = add(low_rank, first[1][size:])
    hop_2(1, low_rank)
    theirs(3, count=1)
    ours(3, count=1)
    hop_3(0, None)
    up, down = second[1]
    low_rank = narrow(low_rank, jnp.where(low, down[size:], up[size:]))
    hop_3(1, low_rank)
    settled = then(add, *third[0])
    own_part = then(add, mine[0, 3], arrived[0, 3])
    up, down = third[1] = then(lambda *t: t, *third[1])
    low_rank = jnp.where(z == 0, down[size:], jnp.where(last_z, up[size:], low_rank))
    moved = jnp.concatenate([settled, add(up[:size], down[:size])], 0)
    base_part = own_part + moved
    return base_part, low_rank.reshape(PIECES * size, -1), second_factors


def shards(
    gate_preactivation,
    up_preactivation,
    base_down_matrix,
    adapter_first_factor,
    adapter_second_factor,
    residual,
    scoring_head_matrix,
    block_adapter_index,
    block_span_start,
    block_span_end,
):
    rows_local, hidden_width = gate_preactivation.shape
    slice_width = residual.shape[1]
    model_width = scoring_head_matrix.shape[0]
    blocks = rows_local // BLOCK
    adapters_here = adapter_first_factor.shape[0]
    data_index = lax.axis_index("dp")
    data_size = lax.axis_size("dp")
    tensor_index = lax.axis_index("tensor")
    on_grid = lax.axis_size("tensor") == LINE * PAIR

    ids = block_adapter_index.reshape(data_size, blocks)
    owner = lax.dynamic_index_in_dim(ids, data_index, 0, keepdims=False) // adapters_here
    first_turned = jnp.swapaxes(adapter_first_factor, 1, 2)
    steps = [step for step in range(1, data_size)] + [0]
    turned = jnp.concatenate(
        [lax.dynamic_slice_in_dim(ids, (data_index + step) % data_size, 1)[0] for step in steps]
    )
    turned = jnp.clip(turned - data_index * adapters_here, 0, adapters_here - 1)
    away = blocks * (data_size - 1)

    def low_rank_terms(rows):
        wanted_first = pick(turned[:away], first_turned)

        def terms(*earlier):
            wanted_second = pick(turned[:away], adapter_second_factor, earlier)
            first_factors = pick(turned[away:], first_turned, earlier)
            second_factors = pick(turned[away:], adapter_second_factor, earlier)
            for n, step in enumerate(steps[:-1]):
                hop = [(d, (d + step) % data_size) for d in range(data_size)]
                take = (owner == (data_index - step) % data_size)[:, None, None]

                def fetched(wanted, kept):
                    came = lax.ppermute(wanted[n * blocks : (n + 1) * blocks], "dp", hop)
                    return jnp.where(take, came, kept)

                first_factors = fetched(wanted_first, first_factors)
                second_factors = fetched(wanted_second, second_factors)
            each = blocks // len(rows)
            product = [
                jnp.einsum(
                    "bcj,bej->bce",
                    part.reshape(each, BLOCK, hidden_width),
                    first_factors[n * each : (n + 1) * each],
                    preferred_element_type=f32,
                ).reshape(each * BLOCK, -1)
                for n, part in enumerate(rows)
            ]
            return jnp.concatenate(product, 0), second_factors

        return wanted_first, terms

    def adapter_delta(low_rank, second_factors):
        return jnp.einsum(
            "bcn,bnt->bct",
            low_rank.astype(bf16).reshape(blocks, BLOCK, -1),
            second_factors,
            preferred_element_type=f32,
        ).reshape(rows_local, slice_width).astype(bf16)

    def hidden_of(gate, up):
        return (jax.nn.silu(gate.astype(f32)) * up.astype(f32)).astype(bf16)

    if on_grid:
        half = rows_local // PIECES
        hidden = [
            hidden_of(gate_preactivation[n * half : (n + 1) * half], up_preactivation[n * half : (n + 1) * half])
            for n in range(PIECES)
        ]
        base_part, low_rank, second_factors = grid_sums(
            hidden, base_down_matrix, tensor_index, slice_width, low_rank_terms
        )
        delta = adapter_delta(low_rank, second_factors)
    else:
        hidden = hidden_of(gate_preactivation, up_preactivation)
        low_rank, second_factors = low_rank_terms([hidden])[1]()
        delta = adapter_delta(lax.psum(low_rank, "tensor"), second_factors)
        base_part = lax.psum_scatter(
            jnp.dot(hidden, base_down_matrix, preferred_element_type=f32),
            "tensor",
            scatter_dimension=1,
            tiled=True,
        )
    combined = residual.astype(f32) + delta.astype(f32) + base_part
    layer_out = combined.astype(bf16)
    head = lax.dynamic_slice_in_dim(
        scoring_head_matrix, tensor_index * slice_width, slice_width
    )
    stats = jnp.stack([jnp.sum(combined * combined, 1), jnp.sum(combined * head[None, :], 1)])
    stats = stats.reshape(2 * blocks, BLOCK)
    stats = exchange_sum(stats, f32) if on_grid else lax.psum(stats, "tensor")
    square_sum, head_sum = stats[:blocks], stats[blocks:]
    scores = head_sum * lax.rsqrt(square_sum / model_width + EPSILON)
    position = jnp.arange(BLOCK, dtype=jnp.int32)
    inside = (position[None, :] >= block_span_start[:, None]) & (
        position[None, :] < block_span_end[:, None]
    )
    span_scores = jnp.sum(jnp.where(inside, scores, f32(0.0)), 1)
    return (layer_out, span_scores)


def solution(mesh):
    return jax.shard_map(
        shards,
        mesh=mesh,
        in_specs=(
            P(("groups", "dp"), "tensor"),
            P(("groups", "dp"), "tensor"),
            P("tensor", None),
            P("dp", "tensor", None),
            P("dp", None, "tensor"),
            P(("groups", "dp"), "tensor"),
            P(),
            P("groups"),
            P(("groups", "dp")),
            P(("groups", "dp")),
        ),
        out_specs=(P(("groups", "dp"), "tensor"), P(("groups", "dp"))),
        check_vma=False,
    )
```

```python
import jax
import jax.numpy as jnp
from jax import lax
from jax.experimental import pallas as pl
from jax.experimental.pallas import tpu as pltpu
from jax.sharding import PartitionSpec as P

BLOCK = 128
EPSILON = 1e-05

f32 = jnp.float32
bf16 = jnp.bfloat16

LINE = 4
PAIR = 2
ORDER = ((3, 2, 1, 0), (0, 3, 2, 1), (1, 0, 3, 2), (0, 1, 2, 3))
PIECES = 2
TILE = 1024

ANYWHERE = pl.BlockSpec(memory_space=pl.ANY)
NO_COST = pl.CostEstimate(flops=0, bytes_accessed=0, transcendentals=0)


def along_line(value, hops):
    pairs = [(a * PAIR + y, b * PAIR + y) for a, b in hops for y in range(PAIR)]
    return lax.ppermute(value, "tensor", pairs)


def across(value, bit):
    size = LINE * PAIR
    return lax.ppermute(value, "tensor", [(t, t ^ bit) for t in range(size)])


def product_kernel(inputs, count, further, index_ref, weights_ref, *refs):
    outs = refs[-count:]
    for n, rows_ref in enumerate(refs[:inputs]):
        result = jnp.dot(rows_ref[...], weights_ref[...], preferred_element_type=f32)
        size = result.shape[0]
        at = 0 if count == inputs else n * size
        ref = outs[n if count == inputs else 0]
        ref[at : at + size] = result.astype(ref.dtype)
        if further:
            ref[size:] = refs[inputs][...].astype(ref.dtype)


def product(hidden, weights, tensor_index, turn, own, kind, width, earlier, piece, count, further=None):
    inputs = hidden if piece is None else hidden[piece : piece + 1]
    rows, depth = inputs[0].shape
    steps = width // TILE
    size = rows * len(inputs) // count
    more = 0 if further is None else further.shape[0]

    def block(j, index):
        z, y = index[0] >> 1, index[0] & 1
        goal = ORDER[LINE - 1][turn]
        for other in range(LINE - 1):
            goal = jnp.where(z == other, ORDER[other][turn], goal)
        return (goal * PAIR + (y if own else 1 - y)) * steps + j

    return pl.pallas_call(
        lambda *refs: product_kernel(len(inputs), count, more, *refs),
        grid_spec=pltpu.PrefetchScalarGridSpec(
            num_scalar_prefetch=1,
            grid=(steps,),
            in_specs=[
                pl.BlockSpec((depth, TILE), lambda j, index: (0, block(j, index))),
            ]
            + [pl.BlockSpec((rows, depth), lambda j, index: (0, 0))] * len(inputs)
            + [pl.BlockSpec((more, TILE), lambda j, index: (0, j))] * (more > 0)
            + [ANYWHERE] * len(earlier),
            out_specs=[pl.BlockSpec((size + more, TILE), lambda j, index: (0, j))] * count,
        ),
        out_shape=[pltpu.HBM((size + more, width), kind)] * count,
        compiler_params=pltpu.CompilerParams(vmem_limit_bytes=40 * 1024 * 1024),
        cost_estimate=NO_COST,
    )(tensor_index.reshape(1), weights, *inputs, *([further] if more else []), *earlier)


def pick_kernel(ids_ref, factors_ref, *refs):
    out_ref, semaphores = refs[-2:]
    copies = [
        pltpu.make_async_copy(factors_ref.at[ids_ref[n]], out_ref.at[n], semaphores.at[n])
        for n in range(out_ref.shape[0])
    ]
    for copy in copies:
        copy.start()
    for copy in copies:
        copy.wait()


def pick(ids, factors, earlier=()):
    shape = ids.shape + factors.shape[1:]
    return pl.pallas_call(
        pick_kernel,
        grid_spec=pltpu.PrefetchScalarGridSpec(
            num_scalar_prefetch=1,
            grid=(1,),
            in_specs=[pl.BlockSpec(memory_space=pltpu.HBM)] + [ANYWHERE] * len(earlier),
            out_specs=pl.BlockSpec(shape, lambda i, ids: (0, 0, 0)),
            scratch_shapes=[pltpu.SemaphoreType.DMA(ids.shape)],
        ),
        out_shape=pltpu.HBM(shape, factors.dtype),
        compiler_params=pltpu.CompilerParams(vmem_limit_bytes=60 * 1024 * 1024),
        cost_estimate=NO_COST,
    )(ids, factors, *earlier)


def exchange_sum(value, wire):
    for bit in (1, 2, 4):
        value = value + across(value.astype(wire), bit).astype(f32)
    return value


UP = ((0, 1), (1, 2), (2, 3))
DOWN = ((3, 2), (2, 1), (1, 0))


class Sequence:
    def __init__(self):
        self.last = None

    def __call__(self, stage, *values):
        if self.last is not None:
            values = lax.optimization_barrier((self.last,) + values)[1:]
        result = stage(*values)
        self.last = jax.tree.leaves(result)[0]
        return result


def grid_sums(hidden, weights, tensor_index, width, low_rank_terms):
    z = tensor_index >> 1
    low, last_z = z < LINE // 2, z == LINE - 1
    pieces = range(PIECES)
    then = Sequence()
    arrived, mine, first, second, third = {}, {}, {}, {}, {}
    add = lambda *terms: sum(t.astype(f32) for t in terms)
    narrow = lambda *terms: add(*terms).astype(bf16)
    size = hidden[0].shape[0]

    def products(k, own, piece, count, further):
        kind = f32 if own else bf16
        out = then(
            lambda w, *more: product(hidden, w, tensor_index, k, own, kind, width, (), piece, count, *more),
            weights,
            *further,
        )
        for p, value in enumerate(out) if piece is None else [(piece, out[0])]:
            if own:
                mine[p, k] = value
            else:
                arrived[p, k] = across(value, 1)

    def theirs(k, *further, piece=None, count=PIECES):
        products(k, False, piece, 1 if piece is not None else count, further)

    def ours(k, piece=None, count=PIECES):
        products(k, True, piece, 1 if piece is not None else count, ())

    def sent(value, further):
        return value if further is None else jnp.concatenate([value, further.astype(bf16)], 0)

    def hop_1(p, further=None):
        value = sent(then(narrow, mine[p, 0], arrived[p, 0][:size]), further)
        first[p] = along_line(value, [UP[0], DOWN[0]])

    def hop_2(p, further=None):
        value = sent(then(narrow, mine[p, 1], arrived[p, 1], first[p][:size]), further)
        second[p] = (along_line(value, UP[:2]), along_line(value, DOWN[:2]))

    def hop_3(p, further):
        def stage(up, down, own, came_own, other, came_other):
            here, there = add(own, came_own), add(other, came_other)
            return narrow(here, up[:size]), narrow(jnp.where(last_z, here, there), down[:size])

        up, down = then(stage, *second[p], mine[p, 2], arrived[p, 2], mine[p, 0], arrived[p, 0][:size])
        third[p] = (along_line(sent(up, further), UP), along_line(sent(down, further), DOWN))

    wanted, low_rank_of = low_rank_terms(hidden)
    hidden[0] = lax.optimization_barrier((wanted, hidden[0]))[1]
    theirs(0, piece=0)
    low_rank, second_factors = low_rank_of()
    low_rank = low_rank.reshape(-1, width)
    theirs(0, low_rank, piece=1)
    ours(0)
    theirs(1, piece=0)
    hop_1(0)
    ours(1)
    theirs(1, piece=1)
    low_rank = add(low_rank, arrived[1, 0][size:])
    hop_1(1, low_rank)
    theirs(2, piece=0)
    ours(2)
    hop_2(0)
    theirs(2, piece=1)
    low_rank = add(low_rank, first[1][size:])
    hop_2(1, low_rank)
    theirs(3, count=1)
    ours(3, count=1)
    hop_3(0, None)
    up, down = second[1]
    low_rank = narrow(low_rank, jnp.where(low, down[size:], up[size:]))
    hop_3(1, low_rank)
    settled = then(add, *third[0])
    own_part = then(add, mine[0, 3], arrived[0, 3])
    up, down = third[1] = then(lambda *t: t, *third[1])
    low_rank = jnp.where(z == 0, down[size:], jnp.where(last_z, up[size:], low_rank))
    moved = jnp.concatenate([settled, add(up[:size], down[:size])], 0)
    base_part = own_part + moved
    return base_part, low_rank.reshape(PIECES * size, -1), second_factors


def shards(
    gate_preactivation,
    up_preactivation,
    base_down_matrix,
    adapter_first_factor,
    adapter_second_factor,
    residual,
    scoring_head_matrix,
    block_adapter_index,
    block_span_start,
    block_span_end,
):
    rows_local, hidden_width = gate_preactivation.shape
    slice_width = residual.shape[1]
    model_width = scoring_head_matrix.shape[0]
    blocks = rows_local // BLOCK
    adapters_here = adapter_first_factor.shape[0]
    data_index = lax.axis_index("dp")
    data_size = lax.axis_size("dp")
    tensor_index = lax.axis_index("tensor")
    on_grid = lax.axis_size("tensor") == LINE * PAIR

    ids = block_adapter_index.reshape(data_size, blocks)
    owner = lax.dynamic_index_in_dim(ids, data_index, 0, keepdims=False) // adapters_here
    first_turned = jnp.swapaxes(adapter_first_factor, 1, 2)
    steps = [step for step in range(1, data_size)] + [0]
    turned = jnp.concatenate(
        [lax.dynamic_slice_in_dim(ids, (data_index + step) % data_size, 1)[0] for step in steps]
    )
    turned = jnp.clip(turned - data_index * adapters_here, 0, adapters_here - 1)
    away = blocks * (data_size - 1)

    def low_rank_terms(rows):
        wanted_first = pick(turned[:away], first_turned)

        def terms(*earlier):
            wanted_second = pick(turned[:away], adapter_second_factor, earlier)
            first_factors = pick(turned[away:], first_turned, earlier)
            second_factors = pick(turned[away:], adapter_second_factor, earlier)
            for n, step in enumerate(steps[:-1]):
                hop = [(d, (d + step) % data_size) for d in range(data_size)]
                take = (owner == (data_index - step) % data_size)[:, None, None]

                def fetched(wanted, kept):
                    came = lax.ppermute(wanted[n * blocks : (n + 1) * blocks], "dp", hop)
                    return jnp.where(take, came, kept)

                first_factors = fetched(wanted_first, first_factors)
                second_factors = fetched(wanted_second, second_factors)
            each = blocks // len(rows)
            product = [
                jnp.einsum(
                    "bcj,bej->bce",
                    part.reshape(each, BLOCK, hidden_width),
                    first_factors[n * each : (n + 1) * each],
                    preferred_element_type=f32,
                ).reshape(each * BLOCK, -1)
                for n, part in enumerate(rows)
            ]
            return jnp.concatenate(product, 0), second_factors

        return wanted_first, terms

    def adapter_delta(low_rank, second_factors):
        return jnp.einsum(
            "bcn,bnt->bct",
            low_rank.astype(bf16).reshape(blocks, BLOCK, -1),
            second_factors,
            preferred_element_type=f32,
        ).reshape(rows_local, slice_width).astype(bf16)

    def hidden_of(gate, up):
        return (jax.nn.silu(gate.astype(f32)) * up.astype(f32)).astype(bf16)

    if on_grid:
        half = rows_local // PIECES
        hidden = [
            hidden_of(gate_preactivation[n * half : (n + 1) * half], up_preactivation[n * half : (n + 1) * half])
            for n in range(PIECES)
        ]
        base_part, low_rank, second_factors = grid_sums(
            hidden, base_down_matrix, tensor_index, slice_width, low_rank_terms
        )
        delta = adapter_delta(low_rank, second_factors)
    else:
        hidden = hidden_of(gate_preactivation, up_preactivation)
        low_rank, second_factors = low_rank_terms([hidden])[1]()
        delta = adapter_delta(lax.psum(low_rank, "tensor"), second_factors)
        base_part = lax.psum_scatter(
            jnp.dot(hidden, base_down_matrix, preferred_element_type=f32),
            "tensor",
            scatter_dimension=1,
            tiled=True,
        )
    combined = residual.astype(f32) + delta.astype(f32) + base_part
    layer_out = combined.astype(bf16)
    head = lax.dynamic_slice_in_dim(
        scoring_head_matrix, tensor_index * slice_width, slice_width
    )
    stats = jnp.stack([jnp.sum(combined * combined, 1), jnp.sum(combined * head[None, :], 1)])
    stats = stats.reshape(2 * blocks, BLOCK)
    stats = exchange_sum(stats, f32) if on_grid else lax.psum(stats, "tensor")
    square_sum, head_sum = stats[:blocks], stats[blocks:]
    scores = head_sum * lax.rsqrt(square_sum / model_width + EPSILON)
    position = jnp.arange(BLOCK, dtype=jnp.int32)
    inside = (position[None, :] >= block_span_start[:, None]) & (
        position[None, :] < block_span_end[:, None]
    )
    span_scores = jnp.sum(jnp.where(inside, scores, f32(0.0)), 1)
    return (layer_out, span_scores)


def solution(mesh):
    return jax.shard_map(
        shards,
        mesh=mesh,
        in_specs=(
            P(("groups", "dp"), "tensor"),
            P(("groups", "dp"), "tensor"),
            P("tensor", None),
            P("dp", "tensor", None),
            P("dp", None, "tensor"),
            P(("groups", "dp"), "tensor"),
            P(),
            P("groups"),
            P(("groups", "dp")),
            P(("groups", "dp")),
        ),
        out_specs=(P(("groups", "dp"), "tensor"), P(("groups", "dp"))),
        check_vma=False,
    )
```
